32 devices in a mesh: groups: 2 (over y), tgt: 4 (over z), src: 2 (over x), sub: 2 (over core).
Axes of the slice: x: 2, y: 2, z: 4, core: 2. Of those that a mesh axis runs over, the one named last changes fastest.
Arguments:
- src_words: int32 [2048], P(('groups', 'tgt', 'src', 'sub')), parts along dimension 0, may hold values from 0 to 12543, as said below
- tgt_words: int32 [2048], P(('groups', 'tgt', 'src', 'sub')), parts along dimension 0, may hold values from 0 to 12543, as said below
- src_vocab: bfloat16 [25088, 300], P(('groups', 'tgt', 'src', 'sub')), parts along dimension 0, may hold values from -3 to 3
- tgt_vocab: bfloat16 [25088, 300], P(('groups', 'tgt', 'src', 'sub')), parts along dimension 0, may hold values from -3 to 3
- mapping: float32 [600, 300], P('groups'), parts along dimension 0, may hold values from -1 to 2
Outputs:
- source_potential: float32 [2048], P(('groups', 'tgt', 'src', 'sub')), parts along dimension 0
- target_potential: float32 [2048], P(('groups', 'tgt', 'src', 'sub')), parts along dimension 0
- rotation: float32 [600, 300], P('groups'), parts along dimension 0
The draws below stay inside these ranges and needn't reach their ends.
There are 2 independent parts, one for each index of `groups`. The reference program is written for one: setup_inputs(seed, part) draws one part's arguments, and reference() takes and returns one part's arrays. A program takes and returns all parts, laid end to end along the dimension named above; each array names one. Nothing has to cross between parts.
Inputs may be any that keep to these rules, and one draw needn't show every extreme that they name: `src_words`: position p names a word of rows q * 784 to (q + 1) * 784 - 1 of the source vocabulary, q = p // 64; in each such block of 64 positions the first names the block's first word and the second its last word. `tgt_words`: position p names a word of rows q * 784 to (q + 1) * 784 - 1 of the target vocabulary, q = p // 64; in each such block of 64 positions the first names the block's first word and the second its last word.
All inputs are finite; a program needn't handle non-finite values.
Results may differ from the reference program's by a relative error of at most 0.0077.
Values may be sent and summed in bfloat16 or wider, within the bound.
No kernel may reach another device: no remote copies, remote signals or barrier semaphores. Data moves between devices by JAX's collectives and lax.ppermute only.
A program may use at most 64 MiB of HBM per device.

```python
import math
import jax
import jax.numpy as jnp
from jax import lax

D = 300
VOCAB_DEV = 784
BD = 64
ITERS = 4
POLAR_STEPS = 8
VOCAB = 12544
B = 1024


def word_ids(key):
    position = jnp.arange(B, dtype=jnp.int32)
    block_index = position // BD
    within = position % BD
    offsets = jax.random.randint(key, (B,), 0, VOCAB_DEV, dtype=jnp.int32)
    offsets = jnp.where(within == 0, 0, jnp.where(within == 1, VOCAB_DEV - 1, offsets))
    return (block_index * VOCAB_DEV + offsets).astype(jnp.int32)


def draw_src_words(key, part):
    return word_ids(jax.random.fold_in(key, 11))


def draw_tgt_words(key, part):
    return word_ids(jax.random.fold_in(key, 12))


def word_vectors(key, salt):
    base = jax.random.fold_in(key, salt)
    key_noise, key_scale = jax.random.split(base, 2)
    scale = jnp.exp(jax.random.uniform(key_scale, (VOCAB, 1), jnp.float32, math.log(0.3), math.log(3.0)))
    root = math.sqrt(D)
    noise = jnp.clip(jax.random.normal(key_noise, (VOCAB, D), jnp.float32), -4.0, 4.0)
    values = scale * noise / root
    return values.astype(jnp.bfloat16)


def draw_src_vocab(key, part):
    return word_vectors(key, 21)


def draw_tgt_vocab(key, part):
    return word_vectors(key, 22)


def draw_mapping(key, part):
    noise = jnp.clip(jax.random.normal(jax.random.fold_in(key, 31), (D, D), jnp.float32), -4.0, 4.0)
    rows = jnp.arange(D)[:, None]
    cols = jnp.arange(D)[None, :]
    ident = jnp.where(rows == cols, 1.0, 0.0).astype(jnp.float32)
    return ident + 0.3 * noise / math.sqrt(D)


def setup_inputs(seed: int = 0, part: int = 0) -> dict:
    splits = jax.random.split(jax.random.key(seed), 6)
    part_splits = jax.random.split(jax.random.fold_in(splits[5], part), 6)
    return {
        "src_words": draw_src_words(jax.random.fold_in(jax.random.fold_in(splits[5], part), 71), part),
        "tgt_words": draw_tgt_words(jax.random.fold_in(jax.random.fold_in(splits[5], part), 71), part),
        "src_vocab": draw_src_vocab(jax.random.fold_in(jax.random.fold_in(splits[5], part), 71), part),
        "tgt_vocab": draw_tgt_vocab(jax.random.fold_in(jax.random.fold_in(splits[5], part), 71), part),
        "mapping": draw_mapping(jax.random.fold_in(jax.random.fold_in(splits[5], part), 71), part),
    }


entropy_scale = 0.05

def reference(src_words, tgt_words, src_vocab, tgt_vocab, mapping):
    highest = lax.Precision.HIGHEST
    xs = jnp.take(src_vocab, src_words, axis=0)
    ys = jnp.take(tgt_vocab, tgt_words, axis=0)
    xw = jnp.dot(xs.astype(jnp.float32), mapping, precision=highest).astype(jnp.bfloat16)
    total = xs.shape[0]
    block = math.gcd(total, 1024)
    nblocks = total // block
    width = xs.shape[1]
    xw_blocks = xw.reshape(nblocks, block, width)
    xs_blocks = xs.reshape(nblocks, block, width)
    ys_t = ys.T
    log_mass = entropy_scale * math.log(1.0 / total)
    log_total = math.log(total)

    def scores_of(rows):
        return jnp.dot(rows, ys_t, preferred_element_type=jnp.float32)
    col_pot = jnp.zeros((total,), jnp.float32)
    row_pot = jnp.zeros((total,), jnp.float32)
    for step in range(ITERS):

        def row_fn(rows, col_pot=col_pot):
            logits = (col_pot[None, :] + scores_of(rows)) / entropy_scale
            peak = lax.optimization_barrier(jnp.max(logits, axis=1))
            return peak + jnp.log(lax.optimization_barrier(jnp.sum(jnp.exp(logits - peak[:, None]), axis=1)))
        row_pot = log_mass - entropy_scale * lax.map(row_fn, xw_blocks).reshape(total)

        def col_fn(carry, inputs):
            peak, mass = carry
            rows, pots = inputs
            logits = (pots[:, None] + scores_of(rows)) / entropy_scale
            block_peak = lax.optimization_barrier(jnp.max(logits, axis=0))
            new_peak = jnp.maximum(peak, block_peak)
            mass = mass * jnp.exp(peak - new_peak) + lax.optimization_barrier(jnp.sum(jnp.exp(logits - new_peak[None, :]), axis=0))
            return ((new_peak, mass), None)
        start = (jnp.full((total,), -jnp.inf, jnp.float32), jnp.zeros((total,), jnp.float32))
        (peak, mass), unused = lax.scan(col_fn, start, (xw_blocks, row_pot.reshape(nblocks, block)))
        col_pot = log_mass - entropy_scale * (peak + jnp.log(mass))

    def cov_fn(carry, inputs):
        rows, source, pots = inputs
        plan = jnp.exp((pots[:, None] + col_pot[None, :] + scores_of(rows)) / entropy_scale + log_total).astype(jnp.bfloat16)
        bary = jnp.dot(plan, ys, preferred_element_type=jnp.float32)
        term = jnp.dot(source.astype(jnp.float32).T, bary, precision=highest)
        return (carry + term, None)
    cov, unused = lax.scan(cov_fn, jnp.zeros((width, width), jnp.float32), (xw_blocks, xs_blocks, row_pot.reshape(nblocks, block)))
    polar = cov / jnp.sqrt(jnp.sum(cov * cov))
    for step in range(POLAR_STEPS):
        square = jnp.dot(polar, polar.T, precision=highest)
        polar = 1.5 * polar - 0.5 * jnp.dot(square, polar, precision=highest)
    rotation = math.sqrt(width) * polar
    return (row_pot, col_pot, rotation)
```

```python
import math

import jax
import jax.numpy as jnp
from jax import lax
from jax.experimental import pallas as pl
from jax.experimental.pallas import tpu as pltpu
from jax.sharding import PartitionSpec as P

ITERS = 4
POLAR_STEPS = 8
LANES = 128
REPLICATED_WORDS = 2048
VMEM_BYTES = 56 * 1024 * 1024

entropy_scale = 0.05

LOG2_SCALE = math.log2(math.e) / entropy_scale


def row_log_total(logits):
    peak = lax.pmax(jnp.max(logits, axis=1), "tgt")
    mass = lax.psum(jnp.sum(jnp.exp(logits - peak[:, None]), axis=1), "tgt")
    return peak + jnp.log(mass)


def col_log_total(logits):
    peak = lax.pmax(jnp.max(logits, axis=0), ("src", "sub"))
    mass = lax.psum(jnp.sum(jnp.exp(logits - peak[None, :]), axis=0), ("src", "sub"))
    return peak + jnp.log(mass)


def tiled_local(src_words, tgt_words, src_vocab, tgt_vocab, mapping):
    highest = lax.Precision.HIGHEST
    vocab_rows = src_vocab.shape[0]
    place = lax.axis_index(("tgt", "src", "sub"))
    own_source = jnp.take(src_vocab, src_words - place * vocab_rows, axis=0)
    own_target = jnp.take(tgt_vocab, tgt_words - place * vocab_rows, axis=0)
    own_projected = jnp.dot(own_source.astype(jnp.float32), mapping, precision=highest).astype(
        jnp.bfloat16
    )
    projected = lax.all_gather(own_projected, "tgt", axis=0, tiled=True)
    target_tile = lax.all_gather(own_target, ("src", "sub"), axis=0, tiled=True)
    scores = jnp.einsum("rd,cd->rc", projected, target_tile, preferred_element_type=jnp.float32)
    local_rows = own_source.shape[0]
    width = own_source.shape[1]
    total = local_rows * lax.axis_size(("tgt", "src", "sub"))
    log_mass = entropy_scale * math.log(1.0 / total)
    log_total = math.log(total)
    col_pot = jnp.zeros((scores.shape[1],), jnp.float32)
    row_pot = jnp.zeros((scores.shape[0],), jnp.float32)
    for step in range(ITERS):
        row_pot = log_mass - entropy_scale * row_log_total(
            (col_pot[None, :] + scores) / entropy_scale
        )
        col_pot = log_mass - entropy_scale * col_log_total(
            (row_pot[:, None] + scores) / entropy_scale
        )
    plan = jnp.exp(
        (row_pot[:, None] + col_pot[None, :] + scores) / entropy_scale + log_total
    ).astype(jnp.bfloat16)
    own_bary = lax.psum_scatter(
        jnp.dot(plan, target_tile, preferred_element_type=jnp.float32),
        "tgt",
        scatter_dimension=0,
        tiled=True,
    )
    partial_cov = jnp.einsum(
        "rd,re->de", own_source.astype(jnp.float32), own_bary, precision=highest
    )
    cov = lax.psum(partial_cov, ("tgt", "src", "sub"))
    polar = cov / jnp.sqrt(jnp.sum(cov * cov))
    for step in range(POLAR_STEPS):
        square = jnp.dot(polar, polar.T, precision=highest)
        polar = 1.5 * polar - 0.5 * jnp.dot(square, polar, precision=highest)
    rotation = math.sqrt(width) * polar
    source_potential = lax.dynamic_slice_in_dim(
        row_pot, lax.axis_index("tgt") * local_rows, local_rows, 0
    )
    target_potential = lax.dynamic_slice_in_dim(
        col_pot, lax.axis_index(("src", "sub")) * local_rows, local_rows, 0
    )
    return (source_potential, target_potential, rotation)


def dot32(a, b):
    return jnp.dot(a, b, preferred_element_type=jnp.float32)


def dot_t(a, b):
    return lax.dot_general(a, b, (((1,), (1,)), ((), ())), preferred_element_type=jnp.float32)


def split(a):
    high = a.astype(jnp.bfloat16)
    low = (a - high.astype(jnp.float32)).astype(jnp.bfloat16)
    return high, low


def pick_kernel(base_ref, src_ids_ref, tgt_ids_ref, src_ref, tgt_ref, out_ref):
    rows, count = src_ids_ref.shape[1], src_ref.shape[0]
    width = src_ref.shape[1]
    head = width // LANES * LANES
    tail = width - head
    base = base_ref[0]
    diag = lax.broadcasted_iota(jnp.int32, (rows, rows), 0) == lax.broadcasted_iota(
        jnp.int32, (rows, rows), 1
    )
    word = lax.broadcasted_iota(jnp.int32, (rows, count), 1)

    def pick(ids_ref, vocab_ref):
        ids = jnp.broadcast_to(ids_ref[...] - base, (rows, rows))
        column = jnp.sum(jnp.where(diag, ids, 0), axis=1, keepdims=True)
        chosen = jnp.where(word == column, 1.0, 0.0).astype(jnp.bfloat16)
        return dot32(chosen, vocab_ref[...]).astype(jnp.bfloat16)

    source = pick(src_ids_ref, src_ref)
    target = pick(tgt_ids_ref, tgt_ref)
    out_ref[:, :head] = source[:, :head]
    out_ref[:, head : head + LANES] = jnp.zeros((rows, LANES), jnp.bfloat16)
    out_ref[:, head : head + tail] = source[:, head:]
    out_ref[:, head + LANES // 2 : head + LANES // 2 + tail] = target[:, head:]
    out_ref[:, head + LANES :] = target[:, :head]


def transport_kernel(masks, place_ref, mapping_ref, *refs):
    blocks = refs[: len(masks)]
    f_ref, g_ref, rot_ref = refs[len(masks) : len(masks) + 3]
    xy_scr, map_hi, map_lo, xw_scr, k_scr, p_scr, m_scr, u_scr, g_scr, ok_scr = refs[
        len(masks) + 3 :
    ]
    local_rows = blocks[0].shape[0]
    n = xy_scr.shape[0]
    width = mapping_ref.shape[0]
    head = width // LANES * LANES
    tail = width - head
    side = head + LANES
    half = LANES // 2
    place = place_ref[0]
    log2n = math.log2(n)
    mass = 1.0 / n
    step_rows = 32
    tiles = n // LANES

    for mask, block in zip(masks, blocks):
        row = pl.multiple_of((place ^ mask) * local_rows, local_rows)
        xy_scr[pl.ds(row, local_rows), :] = block[...]

    hi, lo = split(mapping_ref[...])
    for scr, part in ((map_hi, hi), (map_lo, lo)):
        scr[...] = jnp.zeros_like(scr)
        scr[:width, half : half + tail] = part[:, head:]
        scr[:width, LANES:] = part[:, :head]

    chunk = 256
    ys = xy_scr[:, head:]
    for at in range(0, n, chunk):
        rows = slice(at, at + chunk)
        xs = xy_scr[rows, :side]
        xw = (dot32(xs, map_hi[...]) + dot32(xs, map_lo[...])).astype(jnp.bfloat16)
        xw_scr[rows, :] = xw
        k_scr[rows, :] = dot_t(xw, ys) * LOG2_SCALE

    def lanes(a):
        return [a[:, t * LANES : (t + 1) * LANES] for t in range(tiles)]

    def fold(parts, op):
        parts = list(parts)
        while len(parts) > 1:
            parts = [op(a, b) for a, b in zip(parts[::2], parts[1::2])] + (
                [parts[-1]] if len(parts) % 2 else []
            )
        return parts[0]

    def spread(column):
        return jnp.broadcast_to(column, (column.shape[0], LANES))

    def rows_at(i):
        return pl.ds(pl.multiple_of(i * step_rows, step_rows), step_rows)

    def fold8(parts):
        return [fold([a[s : s + 8] for s in range(0, step_rows, 8)], jnp.add) for a in parts]

    def add_all(acc, parts):
        return tuple(a + b for a, b in zip(acc, fold8(parts)))

    zeros = tuple(jnp.zeros((8, LANES), jnp.float32) for t in range(tiles))
    inf8 = jnp.full((step_rows, LANES), jnp.inf, jnp.float32)

    def first(i, carry):
        acc, low, high = carry
        rows = rows_at(i)
        parts = lanes(k_scr[rows, :])
        peak = spread(jnp.max(fold(parts, jnp.maximum), axis=1, keepdims=True))
        parts = [jnp.exp2(a - peak) for a in parts]
        r = spread(jnp.sum(fold(parts, jnp.add), axis=1, keepdims=True))
        u = mass / r
        for t in range(tiles):
            k_scr[rows, t * LANES : (t + 1) * LANES] = parts[t]
        m_scr[rows, :] = peak
        return add_all(acc, [a * u for a in parts]), jnp.minimum(low, r), jnp.maximum(high, r)

    steps = n // step_rows
    acc, low, high = lax.fori_loop(0, steps, first, (zeros, inf8, -inf8), unroll=2)

    def close(acc):
        return [jnp.broadcast_to(jnp.sum(a, axis=0, keepdims=True), (8, LANES)) for a in acc]

    col = close(acc)
    clow = fold(col, jnp.minimum)
    chigh = fold(col, jnp.maximum)
    for it in range(1, ITERS):
        v = [jnp.concatenate([mass / c] * (step_rows // 8), axis=0) for c in col]
        last = it == ITERS - 1

        def again(i, carry, v=v, last=last):
            acc, low, high = carry
            rows = rows_at(i)
            parts = lanes(k_scr[rows, :])
            r = fold([a * b for a, b in zip(parts, v)], jnp.add)
            r = spread(jnp.sum(r, axis=1, keepdims=True))
            u = mass / r
            if last:
                u_scr[rows, :] = u
                m_scr[rows, :] = -log2n - m_scr[rows, :] - jnp.log2(r)
            return add_all(acc, [a * u for a in parts]), jnp.minimum(low, r), jnp.maximum(high, r)

        acc, low, high = lax.fori_loop(0, steps, again, (zeros, low, high), unroll=2)
        col = close(acc)
        clow = jnp.minimum(clow, fold(col, jnp.minimum))
        chigh = jnp.maximum(chigh, fold(col, jnp.maximum))

    for t in range(tiles):
        g_scr[:, t * LANES : (t + 1) * LANES] = -log2n - jnp.log2(col[t])
    v = [jnp.concatenate([1.0 / c] * (step_rows // 8), axis=0) for c in col]

    def plan_rows(i, carry):
        rows = rows_at(i)
        u = u_scr[rows, :]
        for t, a in enumerate(lanes(k_scr[rows, :])):
            p_scr[rows, t * LANES : (t + 1) * LANES] = (a * u * v[t]).astype(jnp.bfloat16)
        return carry

    lax.fori_loop(0, steps, plan_rows, 0, unroll=2)

    smallest = jnp.minimum(jnp.min(low), jnp.min(clow))
    largest = jnp.maximum(jnp.max(high), jnp.max(chigh))
    safe = jnp.logical_and(smallest >= 2.0**-40, largest <= 2.0**40)

    @pl.when(jnp.logical_not(safe))
    def _():
        for at in range(0, n, chunk):
            rows = slice(at, at + chunk)
            k_scr[rows, :] = dot_t(xw_scr[rows, :], ys) * LOG2_SCALE
        g_scr[...] = jnp.zeros_like(g_scr)

        def row_step(i, carry):
            rows = pl.ds(pl.multiple_of(i * 8, 8), 8)
            logits = k_scr[rows, :] + g_scr[...]
            peak = jnp.max(logits, axis=1, keepdims=True)
            r = jnp.sum(jnp.exp2(logits - peak), axis=1, keepdims=True)
            m_scr[rows, :] = spread(-log2n - peak - jnp.log2(r))
            return carry

        def logits_of(i):
            rows = pl.ds(pl.multiple_of(i * 8, 8), 8)
            return k_scr[rows, :] + jnp.concatenate([m_scr[rows, :]] * tiles, axis=1)

        def iteration(it, carry):
            lax.fori_loop(0, n // 8, row_step, 0)
            peak = lax.fori_loop(
                0,
                n // 8,
                lambda i, a: jnp.maximum(a, logits_of(i)),
                jnp.full((8, n), -jnp.inf, jnp.float32),
            )
            peak = jnp.broadcast_to(jnp.max(peak, axis=0, keepdims=True), (8, n))
            total = lax.fori_loop(
                0,
                n // 8,
                lambda i, a: a + jnp.exp2(logits_of(i) - peak),
                jnp.zeros((8, n), jnp.float32),
            )
            total = jnp.broadcast_to(jnp.sum(total, axis=0, keepdims=True), (8, n))
            g_scr[...] = -log2n - peak - jnp.log2(total)
            return carry

        lax.fori_loop(0, ITERS, iteration, 0)

        def plan_step(i, carry):
            two = [jnp.exp2(logits_of(2 * i + j) + g_scr[...] + log2n) for j in range(2)]
            rows = pl.ds(pl.multiple_of(i * 16, 16), 16)
            p_scr[rows, :] = jnp.concatenate(two, axis=0).astype(jnp.bfloat16)
            return carry

        lax.fori_loop(0, n // 16, plan_step, 0)

    own = pl.ds(pl.multiple_of(place * local_rows, local_rows), local_rows)
    f = m_scr[own, :]
    diag = lax.broadcasted_iota(jnp.int32, f.shape, 0) == lax.broadcasted_iota(
        jnp.int32, f.shape, 1
    )
    f = jnp.sum(jnp.where(diag, f, 0.0), axis=0, keepdims=True) * (1.0 / LOG2_SCALE)
    f_ref[...] = f[:, :local_rows]
    g = pltpu.roll(g_scr[...], lax.rem(n - place * local_rows, n), 1)
    g_ref[...] = g[:1, :local_rows] * (1.0 / LOG2_SCALE)

    deep = (width + 15) // 16 * 16
    cov = jnp.zeros((side, side), jnp.float32)
    for at in range(0, n, chunk):
        rows = slice(at, at + chunk)
        hi, lo = split(dot32(p_scr[rows, :], ys))
        xs_t = xy_scr[rows, :side].T
        cov = cov + dot32(xs_t, hi) + dot32(xs_t, lo)
    cov = cov[:deep]
    place_y = lax.broadcasted_iota(jnp.int32, (deep, side), 1)
    cov = jnp.where(place_y >= half, cov, 0.0)
    q = cov / jnp.sqrt(jnp.sum(cov * cov))
    for step in range(POLAR_STEPS):
        hi, lo = split(q)
        square = dot_t(hi, hi) + dot_t(hi, lo) + dot_t(lo, hi)
        shi, slo = split(square)
        q = 1.5 * q - 0.5 * (dot32(shi, hi) + dot32(shi, lo) + dot32(slo, hi))
    q = q * math.sqrt(width)
    rot_ref[:, :head] = q[:width, LANES:]
    rot_ref[:, head:] = q[:width, half : half + tail]


def gathered_local(src_words, tgt_words, src_vocab, tgt_vocab, mapping):
    axes = ("tgt", "src", "sub")
    sizes = [lax.axis_size(a) for a in axes]
    local_rows = src_words.shape[0]
    vocab_rows, width = src_vocab.shape
    head = width // LANES * LANES
    side = head + LANES
    packed = side + head
    place = lax.axis_index(axes).astype(jnp.int32)
    vmem = pl.BlockSpec(memory_space=pltpu.VMEM)
    smem = pl.BlockSpec(memory_space=pltpu.SMEM)
    own = pl.pallas_call(
        pick_kernel,
        out_shape=jax.ShapeDtypeStruct((local_rows, packed), jnp.bfloat16),
        in_specs=[smem, vmem, vmem, vmem, vmem],
        out_specs=vmem,
        compiler_params=pltpu.CompilerParams(vmem_limit_bytes=VMEM_BYTES),
        name="pick_words",
    )(
        (place * vocab_rows).reshape(1),
        src_words.reshape(1, local_rows),
        tgt_words.reshape(1, local_rows),
        src_vocab,
        tgt_vocab,
    )

    def swap(a, axis, mask):
        return lax.ppermute(a, axis, [(i, i ^ mask) for i in range(lax.axis_size(axis))])

    held = {0: own}
    for axis, below in (("tgt", sizes[1] * sizes[2]), ("src", sizes[2]), ("sub", 1)):
        for mask in range(1, lax.axis_size(axis)):
            for key in [k for k in held if (k // below) % lax.axis_size(axis) == 0]:
                held[key + mask * below] = swap(held[key], axis, mask)
    masks = sorted(held)
    n = local_rows * len(masks)
    f, g, rotation = pl.pallas_call(
        lambda *refs: transport_kernel(masks, *refs),
        out_shape=(
            jax.ShapeDtypeStruct((1, local_rows), jnp.float32),
            jax.ShapeDtypeStruct((1, local_rows), jnp.float32),
            jax.ShapeDtypeStruct((width, width), jnp.float32),
        ),
        in_specs=[smem, vmem] + [vmem] * len(masks),
        out_specs=(vmem, vmem, vmem),
        scratch_shapes=[
            pltpu.VMEM((n, packed), jnp.bfloat16),
            pltpu.VMEM((side, side), jnp.bfloat16),
            pltpu.VMEM((side, side), jnp.bfloat16),
            pltpu.VMEM((n, side), jnp.bfloat16),
            pltpu.VMEM((n, n), jnp.float32),
            pltpu.VMEM((n, n), jnp.bfloat16),
            pltpu.VMEM((n, LANES), jnp.float32),
            pltpu.VMEM((n, LANES), jnp.float32),
            pltpu.VMEM((8, n), jnp.float32),
            pltpu.SMEM((1,), jnp.int32),
        ],
        compiler_params=pltpu.CompilerParams(vmem_limit_bytes=VMEM_BYTES),
        name="transport",
    )(place.reshape(1), mapping, *[held[m] for m in masks])
    return (f.reshape(local_rows), g.reshape(local_rows), rotation)


def local(src_words, tgt_words, src_vocab, tgt_vocab, mapping):
    sizes = [lax.axis_size(a) for a in ("tgt", "src", "sub")]
    local_rows = src_words.shape[0]
    total = local_rows * math.prod(sizes)
    fits = (
        total <= REPLICATED_WORDS
        and total % 256 == 0
        and local_rows % 16 == 0
        and local_rows <= LANES
        and all(s & (s - 1) == 0 for s in sizes)
        and LANES <= src_vocab.shape[1]
        and 0 < src_vocab.shape[1] % LANES <= LANES // 2
    )
    plan = gathered_local if fits else tiled_local
    return plan(src_words, tgt_words, src_vocab, tgt_vocab, mapping)


def solution(mesh):
    placed = (
        P(("groups", "tgt", "src", "sub")),
        P(("groups", "tgt", "src", "sub")),
        P(("groups", "tgt", "src", "sub"), None),
        P(("groups", "tgt", "src", "sub"), None),
        P("groups", None),
    )
    return jax.shard_map(
        local,
        mesh=mesh,
        in_specs=placed,
        out_specs=(
            P(("groups", "tgt", "src", "sub")),
            P(("groups", "tgt", "src", "sub")),
            P("groups", None),
        ),
        check_vma=False,
    )
```

```python
import math

import jax
import jax.numpy as jnp
from jax import lax
from jax.experimental import pallas as pl
from jax.experimental.pallas import tpu as pltpu
from jax.sharding import PartitionSpec as P

ITERS = 4
POLAR_STEPS = 8
LANES = 128
REPLICATED_WORDS = 2048
VMEM_BYTES = 56 * 1024 * 1024
STEP_ROWS = 32

entropy_scale = 0.05

LOG2_SCALE = math.log2(math.e) / entropy_scale


def row_log_total(logits):
    peak = lax.pmax(jnp.max(logits, axis=1), "tgt")
    mass = lax.psum(jnp.sum(jnp.exp(logits - peak[:, None]), axis=1), "tgt")
    return peak + jnp.log(mass)


def col_log_total(logits):
    peak = lax.pmax(jnp.max(logits, axis=0), ("src", "sub"))
    mass = lax.psum(jnp.sum(jnp.exp(logits - peak[None, :]), axis=0), ("src", "sub"))
    return peak + jnp.log(mass)


def tiled_local(src_words, tgt_words, src_vocab, tgt_vocab, mapping):
    highest = lax.Precision.HIGHEST
    vocab_rows = src_vocab.shape[0]
    place = lax.axis_index(("tgt", "src", "sub"))
    own_source = jnp.take(src_vocab, src_words - place * vocab_rows, axis=0)
    own_target = jnp.take(tgt_vocab, tgt_words - place * vocab_rows, axis=0)
    own_projected = jnp.dot(own_source.astype(jnp.float32), mapping, precision=highest).astype(
        jnp.bfloat16
    )
    projected = lax.all_gather(own_projected, "tgt", axis=0, tiled=True)
    target_tile = lax.all_gather(own_target, ("src", "sub"), axis=0, tiled=True)
    scores = jnp.einsum("rd,cd->rc", projected, target_tile, preferred_element_type=jnp.float32)
    local_rows = own_source.shape[0]
    width = own_source.shape[1]
    total = local_rows * lax.axis_size(("tgt", "src", "sub"))
    log_mass = entropy_scale * math.log(1.0 / total)
    log_total = math.log(total)
    col_pot = jnp.zeros((scores.shape[1],), jnp.float32)
    row_pot = jnp.zeros((scores.shape[0],), jnp.float32)
    for step in range(ITERS):
        row_pot = log_mass - entropy_scale * row_log_total(
            (col_pot[None, :] + scores) / entropy_scale
        )
        col_pot = log_mass - entropy_scale * col_log_total(
            (row_pot[:, None] + scores) / entropy_scale
        )
    plan = jnp.exp(
        (row_pot[:, None] + col_pot[None, :] + scores) / entropy_scale + log_total
    ).astype(jnp.bfloat16)
    own_bary = lax.psum_scatter(
        jnp.dot(plan, target_tile, preferred_element_type=jnp.float32),
        "tgt",
        scatter_dimension=0,
        tiled=True,
    )
    partial_cov = jnp.einsum(
        "rd,re->de", own_source.astype(jnp.float32), own_bary, precision=highest
    )
    cov = lax.psum(partial_cov, ("tgt", "src", "sub"))
    polar = cov / jnp.sqrt(jnp.sum(cov * cov))
    for step in range(POLAR_STEPS):
        square = jnp.dot(polar, polar.T, precision=highest)
        polar = 1.5 * polar - 0.5 * jnp.dot(square, polar, precision=highest)
    rotation = math.sqrt(width) * polar
    source_potential = lax.dynamic_slice_in_dim(
        row_pot, lax.axis_index("tgt") * local_rows, local_rows, 0
    )
    target_potential = lax.dynamic_slice_in_dim(
        col_pot, lax.axis_index(("src", "sub")) * local_rows, local_rows, 0
    )
    return (source_potential, target_potential, rotation)


def dot32(a, b):
    return jnp.dot(a, b, preferred_element_type=jnp.float32)


def dot_t(a, b):
    return lax.dot_general(a, b, (((1,), (1,)), ((), ())), preferred_element_type=jnp.float32)


def split(a):
    high = a.astype(jnp.bfloat16)
    low = (a - high.astype(jnp.float32)).astype(jnp.bfloat16)
    return high, low


def pick_kernel(base_ref, src_ids_ref, tgt_ids_ref, src_ref, tgt_ref, out_ref):
    rows = src_ids_ref.shape[1]
    width, count = src_ref.shape
    head = width // LANES * LANES
    tail = width - head
    base = base_ref[0]
    diag = lax.broadcasted_iota(jnp.int32, (rows, rows), 0) == lax.broadcasted_iota(
        jnp.int32, (rows, rows), 1
    )
    word = lax.broadcasted_iota(jnp.int32, (rows, count), 1)

    def pick(ids_ref, vocab_ref):
        ids = jnp.broadcast_to(ids_ref[...] - base, (rows, rows))
        column = jnp.sum(jnp.where(diag, ids, 0), axis=1, keepdims=True)
        chosen = jnp.where(word == column, 1.0, 0.0).astype(jnp.bfloat16)
        return dot_t(chosen, vocab_ref[...]).astype(jnp.bfloat16)

    source = pick(src_ids_ref, src_ref)
    target = pick(tgt_ids_ref, tgt_ref)
    out_ref[:, :head] = source[:, :head]
    out_ref[:, head : head + LANES] = jnp.zeros((rows, LANES), jnp.bfloat16)
    out_ref[:, head : head + tail] = source[:, head:]
    out_ref[:, head + LANES // 2 : head + LANES // 2 + tail] = target[:, head:]
    out_ref[:, head + LANES :] = target[:, :head]


def transport_kernel(masks, place_ref, mapping_ref, *refs):
    blocks = refs[: len(masks)]
    f_ref, g_ref, rot_ref = refs[len(masks) : len(masks) + 3]
    xy_scr, map_hi, map_lo, xw_scr, k_scr, p_scr, m_scr, u_scr, g_scr, ok_scr = refs[
        len(masks) + 3 :
    ]
    local_rows = blocks[0].shape[0]
    n = xy_scr.shape[0]
    width = mapping_ref.shape[0]
    head = width // LANES * LANES
    tail = width - head
    side = head + LANES
    half = LANES // 2
    place = place_ref[0]
    log2n = math.log2(n)
    mass = 1.0 / n
    step_rows = STEP_ROWS
    tiles = n // LANES

    for mask, block in zip(masks, blocks):
        row = pl.multiple_of((place ^ mask) * local_rows, local_rows)
        xy_scr[pl.ds(row, local_rows), :] = block[...]

    hi, lo = split(mapping_ref[...])
    for scr, part in ((map_hi, hi), (map_lo, lo)):
        scr[...] = jnp.zeros_like(scr)
        scr[:width, half : half + tail] = part[:, head:]
        scr[:width, LANES:] = part[:, :head]

    chunk = 256
    ys = xy_scr[:, head:]
    for at in range(0, n, chunk):
        rows = slice(at, at + chunk)
        xs = xy_scr[rows, :side]
        xw = (dot32(xs, map_hi[...]) + dot32(xs, map_lo[...])).astype(jnp.bfloat16)
        xw_scr[rows, :] = xw
        k_scr[rows, :] = dot_t(xw, ys) * LOG2_SCALE

    def lanes(a):
        return [a[:, t * LANES : (t + 1) * LANES] for t in range(tiles)]

    def fold(parts, op):
        parts = list(parts)
        while len(parts) > 1:
            parts = [op(a, b) for a, b in zip(parts[::2], parts[1::2])] + (
                [parts[-1]] if len(parts) % 2 else []
            )
        return parts[0]

    def spread(column):
        return jnp.broadcast_to(column, (column.shape[0], LANES))

    def rows_at(i):
        return pl.ds(pl.multiple_of(i * step_rows, step_rows), step_rows)

    def fold8(parts):
        return [fold([a[s : s + 8] for s in range(0, step_rows, 8)], jnp.add) for a in parts]

    def add_all(acc, parts):
        return tuple(a + b for a, b in zip(acc, fold8(parts)))

    zeros = tuple(jnp.zeros((8, LANES), jnp.float32) for t in range(tiles))
    inf8 = jnp.full((step_rows, LANES), jnp.inf, jnp.float32)

    def first(i, carry):
        acc, low, high = carry
        rows = rows_at(i)
        parts = lanes(k_scr[rows, :])
        peak = spread(jnp.max(fold(parts, jnp.maximum), axis=1, keepdims=True))
        parts = [jnp.exp2(a - peak) for a in parts]
        r = spread(jnp.sum(fold(parts, jnp.add), axis=1, keepdims=True))
        u = mass / r
        for t in range(tiles):
            k_scr[rows, t * LANES : (t + 1) * LANES] = parts[t]
        m_scr[rows, :] = peak
        return add_all(acc, [a * u for a in parts]), jnp.minimum(low, r), jnp.maximum(high, r)

    steps = n // step_rows
    acc, low, high = lax.fori_loop(0, steps, first, (zeros, inf8, -inf8), unroll=True)

    def close(acc):
        return [jnp.broadcast_to(jnp.sum(a, axis=0, keepdims=True), (8, LANES)) for a in acc]

    col = close(acc)
    clow = fold(col, jnp.minimum)
    chigh = fold(col, jnp.maximum)
    for it in range(1, ITERS):
        v = [jnp.concatenate([mass / c] * (step_rows // 8), axis=0) for c in col]
        last = it == ITERS - 1

        def again(i, carry, v=v, last=last):
            acc, low, high = carry
            rows = rows_at(i)
            parts = lanes(k_scr[rows, :])
            r = fold([a * b for a, b in zip(parts, v)], jnp.add)
            r = spread(jnp.sum(r, axis=1, keepdims=True))
            u = mass / r
            if last:
                u_scr[rows, :] = u
                m_scr[rows, :] = -log2n - m_scr[rows, :] - jnp.log2(r)
            return add_all(acc, [a * u for a in parts]), jnp.minimum(low, r), jnp.maximum(high, r)

        acc, low, high = lax.fori_loop(0, steps, again, (zeros, low, high), unroll=True)
        col = close(acc)
        clow = jnp.minimum(clow, fold(col, jnp.minimum))
        chigh = jnp.maximum(chigh, fold(col, jnp.maximum))

    for t in range(tiles):
        g_scr[:, t * LANES : (t + 1) * LANES] = -log2n - jnp.log2(col[t])
    v = [jnp.concatenate([1.0 / c] * (step_rows // 8), axis=0) for c in col]

    def plan_rows(i, carry):
        rows = rows_at(i)
        u = u_scr[rows, :]
        for t, a in enumerate(lanes(k_scr[rows, :])):
            p_scr[rows, t * LANES : (t + 1) * LANES] = (a * u * v[t]).astype(jnp.bfloat16)
        return carry

    lax.fori_loop(0, steps, plan_rows, 0, unroll=True)

    smallest = jnp.minimum(jnp.min(low), jnp.min(clow))
    largest = jnp.maximum(jnp.max(high), jnp.max(chigh))
    safe = jnp.logical_and(smallest >= 2.0**-40, largest <= 2.0**40)

    @pl.when(jnp.logical_not(safe))
    def _():
        for at in range(0, n, chunk):
            rows = slice(at, at + chunk)
            k_scr[rows, :] = dot_t(xw_scr[rows, :], ys) * LOG2_SCALE
        g_scr[...] = jnp.zeros_like(g_scr)

        def row_step(i, carry):
            rows = pl.ds(pl.multiple_of(i * 8, 8), 8)
            logits = k_scr[rows, :] + g_scr[...]
            peak = jnp.max(logits, axis=1, keepdims=True)
            r = jnp.sum(jnp.exp2(logits - peak), axis=1, keepdims=True)
            m_scr[rows, :] = spread(-log2n - peak - jnp.log2(r))
            return carry

        def logits_of(i):
            rows = pl.ds(pl.multiple_of(i * 8, 8), 8)
            return k_scr[rows, :] + jnp.concatenate([m_scr[rows, :]] * tiles, axis=1)

        def iteration(it, carry):
            lax.fori_loop(0, n // 8, row_step, 0)
            peak = lax.fori_loop(
                0,
                n // 8,
                lambda i, a: jnp.maximum(a, logits_of(i)),
                jnp.full((8, n), -jnp.inf, jnp.float32),
            )
            peak = jnp.broadcast_to(jnp.max(peak, axis=0, keepdims=True), (8, n))
            total = lax.fori_loop(
                0,
                n // 8,
                lambda i, a: a + jnp.exp2(logits_of(i) - peak),
                jnp.zeros((8, n), jnp.float32),
            )
            total = jnp.broadcast_to(jnp.sum(total, axis=0, keepdims=True), (8, n))
            g_scr[...] = -log2n - peak - jnp.log2(total)
            return carry

        lax.fori_loop(0, ITERS, iteration, 0)

        def plan_step(i, carry):
            two = [jnp.exp2(logits_of(2 * i + j) + g_scr[...] + log2n) for j in range(2)]
            rows = pl.ds(pl.multiple_of(i * 16, 16), 16)
            p_scr[rows, :] = jnp.concatenate(two, axis=0).astype(jnp.bfloat16)
            return carry

        lax.fori_loop(0, n // 16, plan_step, 0)

    own = pl.ds(pl.multiple_of(place * local_rows, local_rows), local_rows)
    f = m_scr[own, :]
    diag = lax.broadcasted_iota(jnp.int32, f.shape, 0) == lax.broadcasted_iota(
        jnp.int32, f.shape, 1
    )
    f = jnp.sum(jnp.where(diag, f, 0.0), axis=0, keepdims=True) * (1.0 / LOG2_SCALE)
    f_ref[...] = f[:, :local_rows]
    g = pltpu.roll(g_scr[...], lax.rem(n - place * local_rows, n), 1)
    g_ref[...] = g[:1, :local_rows] * (1.0 / LOG2_SCALE)

    deep = (width + 15) // 16 * 16
    cov = jnp.zeros((side, side), jnp.float32)
    for at in range(0, n, chunk):
        rows = slice(at, at + chunk)
        hi, lo = split(dot32(p_scr[rows, :], ys))
        xs_t = xy_scr[rows, :side].T
        cov = cov + dot32(xs_t, hi) + dot32(xs_t, lo)
    cov = cov[:deep]
    place_y = lax.broadcasted_iota(jnp.int32, (deep, side), 1)
    cov = jnp.where(place_y >= half, cov, 0.0)
    q = cov / jnp.sqrt(jnp.sum(cov * cov))
    for step in range(POLAR_STEPS):
        rounded = q.astype(jnp.bfloat16)
        square = dot_t(rounded, rounded).astype(jnp.bfloat16)
        q = 1.5 * q - 0.5 * dot32(square, rounded)
    q = q * math.sqrt(width)
    rot_ref[:, :head] = q[:width, LANES:]
    rot_ref[:, head:] = q[:width, half : half + tail]


def gathered_local(src_words, tgt_words, src_vocab, tgt_vocab, mapping):
    axes = ("tgt", "src", "sub")
    sizes = [lax.axis_size(a) for a in axes]
    local_rows = src_words.shape[0]
    vocab_rows, width = src_vocab.shape
    head = width // LANES * LANES
    side = head + LANES
    packed = side + head
    place = lax.axis_index(axes).astype(jnp.int32)
    vmem = pl.BlockSpec(memory_space=pltpu.VMEM)
    smem = pl.BlockSpec(memory_space=pltpu.SMEM)
    own = pl.pallas_call(
        pick_kernel,
        out_shape=jax.ShapeDtypeStruct((local_rows, packed), jnp.bfloat16),
        in_specs=[smem, vmem, vmem, vmem, vmem],
        out_specs=vmem,
        compiler_params=pltpu.CompilerParams(vmem_limit_bytes=VMEM_BYTES),
        name="pick_words",
    )(
        (place * vocab_rows).reshape(1),
        src_words.reshape(1, local_rows),
        tgt_words.reshape(1, local_rows),
        src_vocab.T,
        tgt_vocab.T,
    )

    def swap(a, axis, mask):
        return lax.ppermute(a, axis, [(i, i ^ mask) for i in range(lax.axis_size(axis))])

    held = {0: own}
    for axis, below in (("tgt", sizes[1] * sizes[2]), ("src", sizes[2]), ("sub", 1)):
        for mask in range(1, lax.axis_size(axis)):
            for key in [k for k in held if (k // below) % lax.axis_size(axis) == 0]:
                held[key + mask * below] = swap(held[key], axis, mask)
    masks = sorted(held)
    n = local_rows * len(masks)
    f, g, rotation = pl.pallas_call(
        lambda *refs: transport_kernel(masks, *refs),
        out_shape=(
            jax.ShapeDtypeStruct((1, local_rows), jnp.float32),
            jax.ShapeDtypeStruct((1, local_rows), jnp.float32),
            jax.ShapeDtypeStruct((width, width), jnp.float32),
        ),
        in_specs=[smem, vmem] + [vmem] * len(masks),
        out_specs=(vmem, vmem, vmem),
        scratch_shapes=[
            pltpu.VMEM((n, packed), jnp.bfloat16),
            pltpu.VMEM((side, side), jnp.bfloat16),
            pltpu.VMEM((side, side), jnp.bfloat16),
            pltpu.VMEM((n, side), jnp.bfloat16),
            pltpu.VMEM((n, n), jnp.float32),
            pltpu.VMEM((n, n), jnp.bfloat16),
            pltpu.VMEM((n, LANES), jnp.float32),
            pltpu.VMEM((n, LANES), jnp.float32),
            pltpu.VMEM((8, n), jnp.float32),
            pltpu.SMEM((1,), jnp.int32),
        ],
        compiler_params=pltpu.CompilerParams(vmem_limit_bytes=VMEM_BYTES),
        name="transport",
    )(place.reshape(1), mapping, *[held[m] for m in masks])
    return (f.reshape(local_rows), g.reshape(local_rows), rotation)


def local(src_words, tgt_words, src_vocab, tgt_vocab, mapping):
    sizes = [lax.axis_size(a) for a in ("tgt", "src", "sub")]
    local_rows = src_words.shape[0]
    total = local_rows * math.prod(sizes)
    fits = (
        total <= REPLICATED_WORDS
        and total % 256 == 0
        and local_rows % 16 == 0
        and local_rows <= LANES
        and all(s & (s - 1) == 0 for s in sizes)
        and LANES <= src_vocab.shape[1]
        and 0 < src_vocab.shape[1] % LANES <= LANES // 2
    )
    plan = gathered_local if fits else tiled_local
    return plan(src_words, tgt_words, src_vocab, tgt_vocab, mapping)


def solution(mesh):
    placed = (
        P(("groups", "tgt", "src", "sub")),
        P(("groups", "tgt", "src", "sub")),
        P(("groups", "tgt", "src", "sub"), None),
        P(("groups", "tgt", "src", "sub"), None),
        P("groups", None),
    )
    return jax.shard_map(
        local,
        mesh=mesh,
        in_specs=placed,
        out_specs=(
            P(("groups", "tgt", "src", "sub")),
            P(("groups", "tgt", "src", "sub")),
            P("groups", None),
        ),
        check_vma=False,
    )
```

```python
import math

import jax
import jax.numpy as jnp
from jax import lax
from jax.experimental import pallas as pl
from jax.experimental.pallas import tpu as pltpu
from jax.sharding import PartitionSpec as P

ITERS = 4
POLAR_STEPS = 8
LANES = 128
REPLICATED_WORDS = 2048
VMEM_BYTES = 56 * 1024 * 1024
KERNEL_VMEM_BYTES = 20 * 1024 * 1024
STEP_ROWS = 32

entropy_scale = 0.05

LOG2_SCALE = math.log2(math.e) / entropy_scale


def row_log_total(logits):
    peak = lax.pmax(jnp.max(logits, axis=1), "tgt")
    mass = lax.psum(jnp.sum(jnp.exp(logits - peak[:, None]), axis=1), "tgt")
    return peak + jnp.log(mass)


def col_log_total(logits):
    peak = lax.pmax(jnp.max(logits, axis=0), ("src", "sub"))
    mass = lax.psum(jnp.sum(jnp.exp(logits - peak[None, :]), axis=0), ("src", "sub"))
    return peak + jnp.log(mass)


def tiled_local(src_words, tgt_words, src_vocab, tgt_vocab, mapping):
    highest = lax.Precision.HIGHEST
    vocab_rows = src_vocab.shape[0]
    place = lax.axis_index(("tgt", "src", "sub"))
    own_source = jnp.take(src_vocab, src_words - place * vocab_rows, axis=0)
    own_target = jnp.take(tgt_vocab, tgt_words - place * vocab_rows, axis=0)
    own_projected = jnp.dot(own_source.astype(jnp.float32), mapping, precision=highest).astype(
        jnp.bfloat16
    )
    projected = lax.all_gather(own_projected, "tgt", axis=0, tiled=True)
    target_tile = lax.all_gather(own_target, ("src", "sub"), axis=0, tiled=True)
    scores = jnp.einsum("rd,cd->rc", projected, target_tile, preferred_element_type=jnp.float32)
    local_rows = own_source.shape[0]
    width = own_source.shape[1]
    total = local_rows * lax.axis_size(("tgt", "src", "sub"))
    log_mass = entropy_scale * math.log(1.0 / total)
    log_total = math.log(total)
    col_pot = jnp.zeros((scores.shape[1],), jnp.float32)
    row_pot = jnp.zeros((scores.shape[0],), jnp.float32)
    for step in range(ITERS):
        row_pot = log_mass - entropy_scale * row_log_total(
            (col_pot[None, :] + scores) / entropy_scale
        )
        col_pot = log_mass - entropy_scale * col_log_total(
            (row_pot[:, None] + scores) / entropy_scale
        )
    plan = jnp.exp(
        (row_pot[:, None] + col_pot[None, :] + scores) / entropy_scale + log_total
    ).astype(jnp.bfloat16)
    own_bary = lax.psum_scatter(
        jnp.dot(plan, target_tile, preferred_element_type=jnp.float32),
        "tgt",
        scatter_dimension=0,
        tiled=True,
    )
    partial_cov = jnp.einsum(
        "rd,re->de", own_source.astype(jnp.float32), own_bary, precision=highest
    )
    cov = lax.psum(partial_cov, ("tgt", "src", "sub"))
    polar = cov / jnp.sqrt(jnp.sum(cov * cov))
    for step in range(POLAR_STEPS):
        square = jnp.dot(polar, polar.T, precision=highest)
        polar = 1.5 * polar - 0.5 * jnp.dot(square, polar, precision=highest)
    rotation = math.sqrt(width) * polar
    source_potential = lax.dynamic_slice_in_dim(
        row_pot, lax.axis_index("tgt") * local_rows, local_rows, 0
    )
    target_potential = lax.dynamic_slice_in_dim(
        col_pot, lax.axis_index(("src", "sub")) * local_rows, local_rows, 0
    )
    return (source_potential, target_potential, rotation)


def dot32(a, b):
    return jnp.dot(a, b, preferred_element_type=jnp.float32)


def dot_t(a, b):
    return lax.dot_general(a, b, (((1,), (1,)), ((), ())), preferred_element_type=jnp.float32)


def split(a):
    high = a.astype(jnp.bfloat16)
    low = (a - high.astype(jnp.float32)).astype(jnp.bfloat16)
    return high, low


def pick_kernel(base_ref, src_ids_ref, tgt_ids_ref, src_ref, tgt_ref, out_ref):
    rows = src_ids_ref.shape[1]
    width, count = src_ref.shape
    head = width // LANES * LANES
    tail = width - head
    base = base_ref[0]
    word = lax.broadcasted_iota(jnp.int32, (count, rows), 0)

    def pick(ids_ref, vocab_ref):
        ids = jnp.broadcast_to(ids_ref[...] - base, (count, rows))
        chosen = jnp.where(word == ids, 1.0, 0.0).astype(jnp.bfloat16)
        return dot32(vocab_ref[...], chosen).T.astype(jnp.bfloat16)

    source = pick(src_ids_ref, src_ref)
    target = pick(tgt_ids_ref, tgt_ref)
    out_ref[:, :head] = source[:, :head]
    out_ref[:, head : head + LANES] = jnp.zeros((rows, LANES), jnp.bfloat16)
    out_ref[:, head : head + tail] = source[:, head:]
    out_ref[:, head + LANES // 2 : head + LANES // 2 + tail] = target[:, head:]
    out_ref[:, head + LANES :] = target[:, :head]


def transport_kernel(masks, place_ref, mapping_ref, *refs):
    blocks = refs[: len(masks)]
    f_ref, g_ref, rot_ref = refs[len(masks) : len(masks) + 3]
    xy_scr, map_hi, map_lo, xw_scr, k_scr, p_scr, m_scr, u_scr, g_scr, cov_scr, sems = refs[
        len(masks) + 3 :
    ]
    local_rows = blocks[0].shape[0]
    n = xy_scr.shape[0]
    width = mapping_ref.shape[0]
    head = width // LANES * LANES
    tail = width - head
    side = head + LANES
    half = LANES // 2
    place = place_ref[0]
    log2n = math.log2(n)
    mass = 1.0 / n
    step_rows = STEP_ROWS
    tiles = n // LANES

    copies = []
    for at, (mask, block) in enumerate(zip(masks, blocks)):
        row = pl.multiple_of((place ^ mask) * local_rows, local_rows)
        copies.append(
            pltpu.make_async_copy(block, xy_scr.at[pl.ds(row, local_rows), :], sems.at[at])
        )
        copies[-1].start()

    hi, lo = split(mapping_ref[...])
    for scr, part in ((map_hi, hi), (map_lo, lo)):
        scr[...] = jnp.zeros_like(scr)
        scr[:width, half : half + tail] = part[:, head:]
        scr[:width, LANES:] = part[:, :head]

    for copy in copies:
        copy.wait()

    chunk = 256
    ys = xy_scr[:, head:]

    def lanes(a):
        return [a[:, t * LANES : (t + 1) * LANES] for t in range(tiles)]

    def fold(parts, op):
        parts = list(parts)
        while len(parts) > 1:
            parts = [op(a, b) for a, b in zip(parts[::2], parts[1::2])] + (
                [parts[-1]] if len(parts) % 2 else []
            )
        return parts[0]

    def spread(column):
        return jnp.broadcast_to(column, (column.shape[0], LANES))

    def rows_at(i):
        return pl.ds(i * step_rows, step_rows)

    def fold8(parts):
        return [fold([a[s : s + 8] for s in range(0, step_rows, 8)], jnp.add) for a in parts]

    def add_all(acc, parts):
        return tuple(a + b for a, b in zip(acc, fold8(parts)))

    zeros = tuple(jnp.zeros((8, LANES), jnp.float32) for t in range(tiles))
    inf8 = jnp.full((step_rows, LANES), jnp.inf, jnp.float32)

    def first(i, carry):
        acc, low, high = carry
        rows = rows_at(i)
        parts = lanes(k_scr[rows, :])
        peak = spread(jnp.max(fold(parts, jnp.maximum), axis=1, keepdims=True))
        parts = [jnp.exp2((a - peak) * LOG2_SCALE) for a in parts]
        r = spread(jnp.sum(fold(parts, jnp.add), axis=1, keepdims=True))
        u = mass / r
        for t in range(tiles):
            k_scr[rows, t * LANES : (t + 1) * LANES] = parts[t]
        m_scr[rows, :] = peak * LOG2_SCALE
        return add_all(acc, [a * u for a in parts]), jnp.minimum(low, r), jnp.maximum(high, r)

    steps = n // step_rows
    carry = (zeros, inf8, -inf8)
    map_all = jnp.concatenate([map_hi[:head], map_lo[:head], map_hi[head:], map_lo[head:]], axis=0)
    for at in range(0, n, chunk):
        rows = slice(at, at + chunk)
        xs = xy_scr[rows, :side]
        sides = [xs[:, :head], xs[:, :head], xs[:, head:], xs[:, head:]]
        xw = dot32(jnp.concatenate(sides, axis=1), map_all).astype(jnp.bfloat16)
        xw_scr[rows, :] = xw
        k_scr[rows, :] = dot_t(xw, ys)
        for i in range(at // step_rows, (at + chunk) // step_rows):
            carry = first(i, carry)
    acc, low, high = carry

    def close(acc):
        return [jnp.broadcast_to(jnp.sum(a, axis=0, keepdims=True), (8, LANES)) for a in acc]

    col = close(acc)
    clow = fold(col, jnp.minimum)
    chigh = fold(col, jnp.maximum)
    for it in range(1, ITERS):
        v = [jnp.concatenate([mass / c] * (step_rows // 8), axis=0) for c in col]
        last = it == ITERS - 1

        def again(i, carry, v=v, last=last):
            acc, low, high = carry
            rows = rows_at(i)
            parts = lanes(k_scr[rows, :])
            r = fold([a * b for a, b in zip(parts, v)], jnp.add)
            r = spread(jnp.sum(r, axis=1, keepdims=True))
            u = mass / r
            if last:
                u_scr[rows, :] = u
                m_scr[rows, :] = -log2n - m_scr[rows, :] - jnp.log2(r)
            return add_all(acc, [a * u for a in parts]), jnp.minimum(low, r), jnp.maximum(high, r)

        carry = (zeros, low, high)
        for i in range(steps):
            carry = again(i, carry)
        acc, low, high = carry
        col = close(acc)
        clow = jnp.minimum(clow, fold(col, jnp.minimum))
        chigh = jnp.maximum(chigh, fold(col, jnp.maximum))

    for t in range(tiles):
        g_scr[:, t * LANES : (t + 1) * LANES] = -log2n - jnp.log2(col[t])
    v = [jnp.concatenate([1.0 / c] * (step_rows // 8), axis=0) for c in col]

    deep = (width + 15) // 16 * 16

    def covariance():
        bary = dot32(p_scr[...], ys).astype(jnp.bfloat16)
        return dot32(xy_scr[:, :side].T, bary)[:deep]

    for i in range(steps):
        rows = rows_at(i)
        u = u_scr[rows, :]
        for t, a in enumerate(lanes(k_scr[rows, :])):
            p_scr[rows, t * LANES : (t + 1) * LANES] = (a * u * v[t]).astype(jnp.bfloat16)
    cov_scr[...] = covariance()

    smallest = jnp.minimum(jnp.min(low), jnp.min(clow))
    largest = jnp.maximum(jnp.max(high), jnp.max(chigh))
    safe = jnp.logical_and(smallest >= 2.0**-40, largest <= 2.0**40)

    @pl.when(jnp.logical_not(safe))
    def _():
        for at in range(0, n, chunk):
            rows = slice(at, at + chunk)
            k_scr[rows, :] = dot_t(xw_scr[rows, :], ys) * LOG2_SCALE
        g_scr[...] = jnp.zeros_like(g_scr)

        def row_step(i, carry):
            rows = pl.ds(pl.multiple_of(i * 8, 8), 8)
            logits = k_scr[rows, :] + g_scr[...]
            peak = jnp.max(logits, axis=1, keepdims=True)
            r = jnp.sum(jnp.exp2(logits - peak), axis=1, keepdims=True)
            m_scr[rows, :] = spread(-log2n - peak - jnp.log2(r))
            return carry

        def logits_of(i):
            rows = pl.ds(pl.multiple_of(i * 8, 8), 8)
            return k_scr[rows, :] + jnp.concatenate([m_scr[rows, :]] * tiles, axis=1)

        def iteration(it, carry):
            lax.fori_loop(0, n // 8, row_step, 0)
            peak = lax.fori_loop(
                0,
                n // 8,
                lambda i, a: jnp.maximum(a, logits_of(i)),
                jnp.full((8, n), -jnp.inf, jnp.float32),
            )
            peak = jnp.broadcast_to(jnp.max(peak, axis=0, keepdims=True), (8, n))
            total = lax.fori_loop(
                0,
                n // 8,
                lambda i, a: a + jnp.exp2(logits_of(i) - peak),
                jnp.zeros((8, n), jnp.float32),
            )
            total = jnp.broadcast_to(jnp.sum(total, axis=0, keepdims=True), (8, n))
            g_scr[...] = -log2n - peak - jnp.log2(total)
            return carry

        lax.fori_loop(0, ITERS, iteration, 0)

        def plan_step(i, carry):
            two = [jnp.exp2(logits_of(2 * i + j) + g_scr[...] + log2n) for j in range(2)]
            rows = pl.ds(pl.multiple_of(i * 16, 16), 16)
            p_scr[rows, :] = jnp.concatenate(two, axis=0).astype(jnp.bfloat16)
            return carry

        lax.fori_loop(0, n // 16, plan_step, 0)
        cov_scr[...] = covariance()

    own = pl.ds(pl.multiple_of(place * local_rows, local_rows), local_rows)
    f = m_scr[own, :]
    diag = lax.broadcasted_iota(jnp.int32, f.shape, 0) == lax.broadcasted_iota(
        jnp.int32, f.shape, 1
    )
    f = jnp.sum(jnp.where(diag, f, 0.0), axis=0, keepdims=True) * (1.0 / LOG2_SCALE)
    f_ref[...] = f[:, :local_rows]
    g = pltpu.roll(g_scr[...], lax.rem(n - place * local_rows, n), 1)
    g_ref[...] = g[:1, :local_rows] * (1.0 / LOG2_SCALE)

    cov = cov_scr[...]
    place_y = lax.broadcasted_iota(jnp.int32, (deep, side), 1)
    cov = jnp.where(place_y >= half, cov, 0.0)
    q = cov / jnp.sqrt(jnp.sum(cov * cov))
    for step in range(POLAR_STEPS):
        rounded = q.astype(jnp.bfloat16)
        square = dot_t(rounded, rounded).astype(jnp.bfloat16)
        q = 1.5 * q - 0.5 * dot32(square, rounded)
    q = q * math.sqrt(width)
    rot_ref[:, :head] = q[:width, LANES:]
    rot_ref[:, head:] = q[:width, half : half + tail]


def gathered_local(src_words, tgt_words, src_vocab, tgt_vocab, mapping):
    axes = ("tgt", "src", "sub")
    sizes = [lax.axis_size(a) for a in axes]
    local_rows = src_words.shape[0]
    vocab_rows, width = src_vocab.shape
    head = width // LANES * LANES
    side = head + LANES
    packed = side + head
    place = lax.axis_index(axes).astype(jnp.int32)
    vmem = pl.BlockSpec(memory_space=pltpu.VMEM)
    smem = pl.BlockSpec(memory_space=pltpu.SMEM)
    own = pl.pallas_call(
        pick_kernel,
        out_shape=jax.ShapeDtypeStruct((local_rows, packed), jnp.bfloat16),
        in_specs=[smem, vmem, vmem, vmem, vmem],
        out_specs=vmem,
        compiler_params=pltpu.CompilerParams(vmem_limit_bytes=VMEM_BYTES),
        name="pick_words",
    )(
        (place * vocab_rows).reshape(1),
        src_words.reshape(1, local_rows),
        tgt_words.reshape(1, local_rows),
        src_vocab.T,
        tgt_vocab.T,
    )

    def swap(a, axis, mask):
        return lax.ppermute(a, axis, [(i, i ^ mask) for i in range(lax.axis_size(axis))])

    held = {0: own}
    for axis, below in (("tgt", sizes[1] * sizes[2]), ("src", sizes[2]), ("sub", 1)):
        for mask in range(1, lax.axis_size(axis)):
            for key in [k for k in held if (k // below) % lax.axis_size(axis) == 0]:
                held[key + mask * below] = swap(held[key], axis, mask)
    masks = sorted(held)
    n = local_rows * len(masks)
    f, g, rotation = pl.pallas_call(
        lambda *refs: transport_kernel(masks, *refs),
        out_shape=(
            jax.ShapeDtypeStruct((1, local_rows), jnp.float32),
            jax.ShapeDtypeStruct((1, local_rows), jnp.float32),
            jax.ShapeDtypeStruct((width, width), jnp.float32),
        ),
        in_specs=[smem, vmem] + [pl.BlockSpec(memory_space=pl.ANY)] * len(masks),
        out_specs=(vmem, vmem, vmem),
        scratch_shapes=[
            pltpu.VMEM((n, packed), jnp.bfloat16),
            pltpu.VMEM((side, side), jnp.bfloat16),
            pltpu.VMEM((side, side), jnp.bfloat16),
            pltpu.VMEM((n, side), jnp.bfloat16),
            pltpu.VMEM((n, n), jnp.float32),
            pltpu.VMEM((n, n), jnp.bfloat16),
            pltpu.VMEM((n, LANES), jnp.float32),
            pltpu.VMEM((n, LANES), jnp.float32),
            pltpu.VMEM((8, n), jnp.float32),
            pltpu.VMEM(((width + 15) // 16 * 16, side), jnp.float32),
            pltpu.SemaphoreType.DMA((len(masks),)),
        ],
        compiler_params=pltpu.CompilerParams(vmem_limit_bytes=KERNEL_VMEM_BYTES),
        name="transport",
    )(place.reshape(1), mapping, *[held[m] for m in masks])
    return (f.reshape(local_rows), g.reshape(local_rows), rotation)


def local(src_words, tgt_words, src_vocab, tgt_vocab, mapping):
    sizes = [lax.axis_size(a) for a in ("tgt", "src", "sub")]
    local_rows = src_words.shape[0]
    total = local_rows * math.prod(sizes)
    fits = (
        total <= REPLICATED_WORDS
        and total % 256 == 0
        and local_rows % 16 == 0
        and local_rows <= LANES
        and all(s & (s - 1) == 0 for s in sizes)
        and LANES <= src_vocab.shape[1]
        and 0 < src_vocab.shape[1] % LANES <= LANES // 2
    )
    plan = gathered_local if fits else tiled_local
    return plan(src_words, tgt_words, src_vocab, tgt_vocab, mapping)


def solution(mesh):
    placed = (
        P(("groups", "tgt", "src", "sub")),
        P(("groups", "tgt", "src", "sub")),
        P(("groups", "tgt", "src", "sub"), None),
        P(("groups", "tgt", "src", "sub"), None),
        P("groups", None),
    )
    return jax.shard_map(
        local,
        mesh=mesh,
        in_specs=placed,
        out_specs=(
            P(("groups", "tgt", "src", "sub")),
            P(("groups", "tgt", "src", "sub")),
            P("groups", None),
        ),
        check_vma=False,
    )
```

```python
import math

import jax
import jax.numpy as jnp
from jax import lax
from jax.experimental import pallas as pl
from jax.experimental.pallas import tpu as pltpu
from jax.sharding import PartitionSpec as P

ITERS = 4
POLAR_STEPS = 8
LANES = 128
REPLICATED_WORDS = 2048
VMEM_BYTES = 56 * 1024 * 1024
KERNEL_VMEM_BYTES = 20 * 1024 * 1024
STEP_ROWS = 32

entropy_scale = 0.05

LOG2_SCALE = math.log2(math.e) / entropy_scale


def row_log_total(logits):
    peak = lax.pmax(jnp.max(logits, axis=1), "tgt")
    mass = lax.psum(jnp.sum(jnp.exp(logits - peak[:, None]), axis=1), "tgt")
    return peak + jnp.log(mass)


def col_log_total(logits):
    peak = lax.pmax(jnp.max(logits, axis=0), ("src", "sub"))
    mass = lax.psum(jnp.sum(jnp.exp(logits - peak[None, :]), axis=0), ("src", "sub"))
    return peak + jnp.log(mass)


def tiled_local(src_words, tgt_words, src_vocab, tgt_vocab, mapping):
    highest = lax.Precision.HIGHEST
    vocab_rows = src_vocab.shape[0]
    place = lax.axis_index(("tgt", "src", "sub"))
    own_source = jnp.take(src_vocab, src_words - place * vocab_rows, axis=0)
    own_target = jnp.take(tgt_vocab, tgt_words - place * vocab_rows, axis=0)
    own_projected = jnp.dot(own_source.astype(jnp.float32), mapping, precision=highest).astype(
        jnp.bfloat16
    )
    projected = lax.all_gather(own_projected, "tgt", axis=0, tiled=True)
    target_tile = lax.all_gather(own_target, ("src", "sub"), axis=0, tiled=True)
    scores = jnp.einsum("rd,cd->rc", projected, target_tile, preferred_element_type=jnp.float32)
    local_rows = own_source.shape[0]
    width = own_source.shape[1]
    total = local_rows * lax.axis_size(("tgt", "src", "sub"))
    log_mass = entropy_scale * math.log(1.0 / total)
    log_total = math.log(total)
    col_pot = jnp.zeros((scores.shape[1],), jnp.float32)
    row_pot = jnp.zeros((scores.shape[0],), jnp.float32)
    for step in range(ITERS):
        row_pot = log_mass - entropy_scale * row_log_total(
            (col_pot[None, :] + scores) / entropy_scale
        )
        col_pot = log_mass - entropy_scale * col_log_total(
            (row_pot[:, None] + scores) / entropy_scale
        )
    plan = jnp.exp(
        (row_pot[:, None] + col_pot[None, :] + scores) / entropy_scale + log_total
    ).astype(jnp.bfloat16)
    own_bary = lax.psum_scatter(
        jnp.dot(plan, target_tile, preferred_element_type=jnp.float32),
        "tgt",
        scatter_dimension=0,
        tiled=True,
    )
    partial_cov = jnp.einsum(
        "rd,re->de", own_source.astype(jnp.float32), own_bary, precision=highest
    )
    cov = lax.psum(partial_cov, ("tgt", "src", "sub"))
    polar = cov / jnp.sqrt(jnp.sum(cov * cov))
    for step in range(POLAR_STEPS):
        square = jnp.dot(polar, polar.T, precision=highest)
        polar = 1.5 * polar - 0.5 * jnp.dot(square, polar, precision=highest)
    rotation = math.sqrt(width) * polar
    source_potential = lax.dynamic_slice_in_dim(
        row_pot, lax.axis_index("tgt") * local_rows, local_rows, 0
    )
    target_potential = lax.dynamic_slice_in_dim(
        col_pot, lax.axis_index(("src", "sub")) * local_rows, local_rows, 0
    )
    return (source_potential, target_potential, rotation)


def dot32(a, b):
    return jnp.dot(a, b, preferred_element_type=jnp.float32)


def dot_t(a, b):
    return lax.dot_general(a, b, (((1,), (1,)), ((), ())), preferred_element_type=jnp.float32)


def split(a):
    high = a.astype(jnp.bfloat16)
    low = (a - high.astype(jnp.float32)).astype(jnp.bfloat16)
    return high, low


def pick_kernel(base_ref, src_ids_ref, tgt_ids_ref, src_ref, tgt_ref, out_ref):
    rows = src_ids_ref.shape[1]
    width, count = src_ref.shape
    head = width // LANES * LANES
    tail = width - head
    base = base_ref[0]
    word = lax.broadcasted_iota(jnp.int32, (count, rows), 0)

    def pick(ids_ref, vocab_ref):
        ids = jnp.broadcast_to(ids_ref[...] - base, (count, rows))
        chosen = jnp.where(word == ids, 1.0, 0.0).astype(jnp.bfloat16)
        return dot32(vocab_ref[...], chosen).T.astype(jnp.bfloat16)

    source = pick(src_ids_ref, src_ref)
    target = pick(tgt_ids_ref, tgt_ref)
    out_ref[:, :head] = source[:, :head]
    out_ref[:, head : head + LANES] = jnp.zeros((rows, LANES), jnp.bfloat16)
    out_ref[:, head : head + tail] = source[:, head:]
    out_ref[:, head + LANES // 2 : head + LANES // 2 + tail] = target[:, head:]
    out_ref[:, head + LANES :] = target[:, :head]


def map_kernel(mapping_ref, out_ref):
    width = mapping_ref.shape[0]
    head = width // LANES * LANES
    half = LANES // 2
    tail = width - head
    out_ref[...] = jnp.zeros_like(out_ref)
    for at, part in enumerate(split(mapping_ref[...])):
        top, low = head * at, head * 2 + LANES * at
        for row, rows in ((top, part[:head]), (low, part[head:])):
            count = rows.shape[0]
            out_ref[row : row + count, half : half + tail] = rows[:, head:]
            out_ref[row : row + count, LANES:] = rows[:, :head]


def transport_kernel(masks, place_ref, map_ref, *refs):
    blocks = refs[: len(masks)]
    f_ref, g_ref, rot_ref = refs[len(masks) : len(masks) + 3]
    xy_scr, xw_scr, k_scr, p_scr, m_scr, u_scr, g_scr, cov_scr, sems = refs[
        len(masks) + 3 :
    ]
    local_rows = blocks[0].shape[0]
    n = xy_scr.shape[0]
    width = rot_ref.shape[0]
    head = width // LANES * LANES
    tail = width - head
    side = head + LANES
    half = LANES // 2
    place = place_ref[0]
    log2n = math.log2(n)
    mass = 1.0 / n
    step_rows = STEP_ROWS
    tiles = n // LANES

    copies = []
    for at, (mask, block) in enumerate(zip(masks, blocks)):
        row = pl.multiple_of((place ^ mask) * local_rows, local_rows)
        copies.append(
            pltpu.make_async_copy(block, xy_scr.at[pl.ds(row, local_rows), :], sems.at[at])
        )
        copies[-1].start()

    for copy in copies:
        copy.wait()

    chunk = 256
    ys = xy_scr[:, head:]

    def lanes(a):
        return [a[:, t * LANES : (t + 1) * LANES] for t in range(tiles)]

    def fold(parts, op):
        parts = list(parts)
        while len(parts) > 1:
            parts = [op(a, b) for a, b in zip(parts[::2], parts[1::2])] + (
                [parts[-1]] if len(parts) % 2 else []
            )
        return parts[0]

    def spread(column):
        return jnp.broadcast_to(column, (column.shape[0], LANES))

    def rows_at(i):
        return pl.ds(i * step_rows, step_rows)

    def fold8(parts):
        return [fold([a[s : s + 8] for s in range(0, step_rows, 8)], jnp.add) for a in parts]

    def add_all(acc, parts):
        return tuple(a + b for a, b in zip(acc, fold8(parts)))

    zeros = tuple(jnp.zeros((8, LANES), jnp.float32) for t in range(tiles))
    inf8 = jnp.full((step_rows, LANES), jnp.inf, jnp.float32)

    def first(i, carry):
        acc, low, high = carry
        rows = rows_at(i)
        parts = lanes(k_scr[rows, :])
        peak = spread(jnp.max(fold(parts, jnp.maximum), axis=1, keepdims=True))
        parts = [jnp.exp2((a - peak) * LOG2_SCALE) for a in parts]
        r = spread(jnp.sum(fold(parts, jnp.add), axis=1, keepdims=True))
        u = mass / r
        for t in range(tiles):
            k_scr[rows, t * LANES : (t + 1) * LANES] = parts[t]
        m_scr[rows, :] = peak * LOG2_SCALE
        return add_all(acc, [a * u for a in parts]), jnp.minimum(low, r), jnp.maximum(high, r)

    steps = n // step_rows
    carry = (zeros, inf8, -inf8)
    map_all = map_ref[...]
    for at in range(0, n, chunk):
        rows = slice(at, at + chunk)
        xs = xy_scr[rows, :side]
        sides = [xs[:, :head], xs[:, :head], xs[:, head:], xs[:, head:]]
        xw = dot32(jnp.concatenate(sides, axis=1), map_all).astype(jnp.bfloat16)
        xw_scr[rows, :] = xw
        k_scr[rows, :] = dot_t(xw, ys)
        for i in range(at // step_rows, (at + chunk) // step_rows):
            carry = first(i, carry)
    acc, low, high = carry

    def close(acc):
        return [jnp.broadcast_to(jnp.sum(a, axis=0, keepdims=True), (8, LANES)) for a in acc]

    col = close(acc)
    clow = fold(col, jnp.minimum)
    chigh = fold(col, jnp.maximum)
    for it in range(1, ITERS):
        v = [jnp.concatenate([mass / c] * (step_rows // 8), axis=0) for c in col]
        last = it == ITERS - 1

        def again(i, carry, v=v, last=last):
            acc, low, high = carry
            rows = rows_at(i)
            parts = lanes(k_scr[rows, :])
            r = fold([a * b for a, b in zip(parts, v)], jnp.add)
            r = spread(jnp.sum(r, axis=1, keepdims=True))
            u = mass / r
            if last:
                u_scr[rows, :] = u
                m_scr[rows, :] = -log2n - m_scr[rows, :] - jnp.log2(r)
            return add_all(acc, [a * u for a in parts]), jnp.minimum(low, r), jnp.maximum(high, r)

        carry = (zeros, low, high)
        for i in range(steps):
            carry = again(i, carry)
        acc, low, high = carry
        col = close(acc)
        clow = jnp.minimum(clow, fold(col, jnp.minimum))
        chigh = jnp.maximum(chigh, fold(col, jnp.maximum))

    for t in range(tiles):
        g_scr[:, t * LANES : (t + 1) * LANES] = -log2n - jnp.log2(col[t])
    v = [jnp.concatenate([1.0 / c] * (step_rows // 8), axis=0) for c in col]

    deep = (width + 15) // 16 * 16

    def covariance():
        bary = dot32(p_scr[...], ys).astype(jnp.bfloat16)
        return dot32(xy_scr[:, :side].T, bary)[:deep]

    for i in range(steps):
        rows = rows_at(i)
        u = u_scr[rows, :]
        for t, a in enumerate(lanes(k_scr[rows, :])):
            p_scr[rows, t * LANES : (t + 1) * LANES] = (a * u * v[t]).astype(jnp.bfloat16)
    cov_scr[...] = covariance()

    smallest = jnp.minimum(jnp.min(low), jnp.min(clow))
    largest = jnp.maximum(jnp.max(high), jnp.max(chigh))
    safe = jnp.logical_and(smallest >= 2.0**-40, largest <= 2.0**40)

    @pl.when(jnp.logical_not(safe))
    def _():
        for at in range(0, n, chunk):
            rows = slice(at, at + chunk)
            k_scr[rows, :] = dot_t(xw_scr[rows, :], ys) * LOG2_SCALE
        g_scr[...] = jnp.zeros_like(g_scr)

        def row_step(i, carry):
            rows = pl.ds(pl.multiple_of(i * 8, 8), 8)
            logits = k_scr[rows, :] + g_scr[...]
            peak = jnp.max(logits, axis=1, keepdims=True)
            r = jnp.sum(jnp.exp2(logits - peak), axis=1, keepdims=True)
            m_scr[rows, :] = spread(-log2n - peak - jnp.log2(r))
            return carry

        def logits_of(i):
            rows = pl.ds(pl.multiple_of(i * 8, 8), 8)
            return k_scr[rows, :] + jnp.concatenate([m_scr[rows, :]] * tiles, axis=1)

        def iteration(it, carry):
            lax.fori_loop(0, n // 8, row_step, 0)
            peak = lax.fori_loop(
                0,
                n // 8,
                lambda i, a: jnp.maximum(a, logits_of(i)),
                jnp.full((8, n), -jnp.inf, jnp.float32),
            )
            peak = jnp.broadcast_to(jnp.max(peak, axis=0, keepdims=True), (8, n))
            total = lax.fori_loop(
                0,
                n // 8,
                lambda i, a: a + jnp.exp2(logits_of(i) - peak),
                jnp.zeros((8, n), jnp.float32),
            )
            total = jnp.broadcast_to(jnp.sum(total, axis=0, keepdims=True), (8, n))
            g_scr[...] = -log2n - peak - jnp.log2(total)
            return carry

        lax.fori_loop(0, ITERS, iteration, 0)

        def plan_step(i, carry):
            two = [jnp.exp2(logits_of(2 * i + j) + g_scr[...] + log2n) for j in range(2)]
            rows = pl.ds(pl.multiple_of(i * 16, 16), 16)
            p_scr[rows, :] = jnp.concatenate(two, axis=0).astype(jnp.bfloat16)
            return carry

        lax.fori_loop(0, n // 16, plan_step, 0)
        cov_scr[...] = covariance()

    own = pl.ds(pl.multiple_of(place * local_rows, local_rows), local_rows)
    f = m_scr[own, :]
    diag = lax.broadcasted_iota(jnp.int32, f.shape, 0) == lax.broadcasted_iota(
        jnp.int32, f.shape, 1
    )
    f = jnp.sum(jnp.where(diag, f, 0.0), axis=0, keepdims=True) * (1.0 / LOG2_SCALE)
    f_ref[...] = f[:, :local_rows]
    g = pltpu.roll(g_scr[...], lax.rem(n - place * local_rows, n), 1)
    g_ref[...] = g[:1, :local_rows] * (1.0 / LOG2_SCALE)

    cov = cov_scr[...]
    place_y = lax.broadcasted_iota(jnp.int32, (deep, side), 1)
    cov = jnp.where(place_y >= half, cov, 0.0)
    q = cov / jnp.sqrt(jnp.sum(cov * cov))
    for step in range(POLAR_STEPS):
        rounded = q.astype(jnp.bfloat16)
        square = dot_t(rounded, rounded).astype(jnp.bfloat16)
        q = 1.5 * q - 0.5 * dot32(square, rounded)
    q = q * math.sqrt(width)
    rot_ref[:, :head] = q[:width, LANES:]
    rot_ref[:, head:] = q[:width, half : half + tail]


def gathered_local(src_words, tgt_words, src_vocab, tgt_vocab, mapping):
    axes = ("tgt", "src", "sub")
    sizes = [lax.axis_size(a) for a in axes]
    local_rows = src_words.shape[0]
    vocab_rows, width = src_vocab.shape
    head = width // LANES * LANES
    side = head + LANES
    packed = side + head
    place = lax.axis_index(axes).astype(jnp.int32)
    vmem = pl.BlockSpec(memory_space=pltpu.VMEM)
    smem = pl.BlockSpec(memory_space=pltpu.SMEM)
    own = pl.pallas_call(
        pick_kernel,
        out_shape=jax.ShapeDtypeStruct((local_rows, packed), jnp.bfloat16),
        in_specs=[smem, vmem, vmem, vmem, vmem],
        out_specs=vmem,
        compiler_params=pltpu.CompilerParams(vmem_limit_bytes=VMEM_BYTES),
        name="pick_words",
    )(
        (place * vocab_rows).reshape(1),
        src_words.reshape(1, local_rows),
        tgt_words.reshape(1, local_rows),
        src_vocab.T,
        tgt_vocab.T,
    )

    def swap(a, axis, mask):
        return lax.ppermute(a, axis, [(i, i ^ mask) for i in range(lax.axis_size(axis))])

    held = {0: own}
    for axis, below in (("tgt", sizes[1] * sizes[2]), ("src", sizes[2]), ("sub", 1)):
        for mask in range(1, lax.axis_size(axis)):
            for key in [k for k in held if (k // below) % lax.axis_size(axis) == 0]:
                held[key + mask * below] = swap(held[key], axis, mask)
    masks = sorted(held)
    middle = masks[min(len(masks) // 2 + sizes[2], len(masks) - 1)]
    mapping, held[middle] = lax.optimization_barrier((mapping, held[middle]))
    halves = pl.pallas_call(
        map_kernel,
        out_shape=jax.ShapeDtypeStruct((2 * side, side), jnp.bfloat16),
        in_specs=[vmem],
        out_specs=vmem,
        compiler_params=pltpu.CompilerParams(vmem_limit_bytes=4 * 1024 * 1024),
        name="map_halves",
    )(mapping)
    n = local_rows * len(masks)
    f, g, rotation = pl.pallas_call(
        lambda *refs: transport_kernel(masks, *refs),
        out_shape=(
            jax.ShapeDtypeStruct((1, local_rows), jnp.float32),
            jax.ShapeDtypeStruct((1, local_rows), jnp.float32),
            jax.ShapeDtypeStruct((width, width), jnp.float32),
        ),
        in_specs=[smem, vmem] + [pl.BlockSpec(memory_space=pl.ANY)] * len(masks),
        out_specs=(vmem, vmem, vmem),
        scratch_shapes=[
            pltpu.VMEM((n, packed), jnp.bfloat16),
            pltpu.VMEM((n, side), jnp.bfloat16),
            pltpu.VMEM((n, n), jnp.float32),
            pltpu.VMEM((n, n), jnp.bfloat16),
            pltpu.VMEM((n, LANES), jnp.float32),
            pltpu.VMEM((n, LANES), jnp.float32),
            pltpu.VMEM((8, n), jnp.float32),
            pltpu.VMEM(((width + 15) // 16 * 16, side), jnp.float32),
            pltpu.SemaphoreType.DMA((len(masks),)),
        ],
        compiler_params=pltpu.CompilerParams(vmem_limit_bytes=KERNEL_VMEM_BYTES),
        name="transport",
    )(place.reshape(1), halves, *[held[m] for m in masks])
    return (f.reshape(local_rows), g.reshape(local_rows), rotation)


def local(src_words, tgt_words, src_vocab, tgt_vocab, mapping):
    sizes = [lax.axis_size(a) for a in ("tgt", "src", "sub")]
    local_rows = src_words.shape[0]
    total = local_rows * math.prod(sizes)
    fits = (
        total <= REPLICATED_WORDS
        and total % 256 == 0
        and local_rows % 16 == 0
        and local_rows <= LANES
        and all(s & (s - 1) == 0 for s in sizes)
        and LANES <= src_vocab.shape[1]
        and 0 < src_vocab.shape[1] % LANES <= LANES // 2
    )
    plan = gathered_local if fits else tiled_local
    return plan(src_words, tgt_words, src_vocab, tgt_vocab, mapping)


def solution(mesh):
    placed = (
        P(("groups", "tgt", "src", "sub")),
        P(("groups", "tgt", "src", "sub")),
        P(("groups", "tgt", "src", "sub"), None),
        P(("groups", "tgt", "src", "sub"), None),
        P("groups", None),
    )
    return jax.shard_map(
        local,
        mesh=mesh,
        in_specs=placed,
        out_specs=(
            P(("groups", "tgt", "src", "sub")),
            P(("groups", "tgt", "src", "sub")),
            P("groups", None),
        ),
        check_vma=False,
    )
```
